32 devices in a mesh: dof: 1, tm: 32 (over z, y, x, core).
Axes of the slice: x: 2, y: 2, z: 4, core: 2. Of those that a mesh axis runs over, the one named last changes fastest.
Arguments:
- snapshots: bfloat16 [8192, 2048], P('dof', 'tm')
- derivatives: bfloat16 [8192, 2048], P('dof', 'tm')
- basis: bfloat16 [8192, 512], P('dof'), may hold values from -0.0625 to 0.0625
Outputs:
- states: float32 [512, 2048], P('dof', 'tm')
- operator: float32 [512, 512], P('dof')
The draws below stay inside these ranges and needn't reach their ends.
All inputs are finite; a program needn't handle non-finite values.
Results may differ from the reference program's by a relative error of at most 0.0003.
Values sent between devices are 32-bit elements; how exact they have to be, the bound alone decides.
A program may use at most 64 MiB of HBM per device.

```python
import jax
import jax.numpy as jnp
from jax import lax

R = 512
NDOF = 8192
NSNAP = 2048


def shared_field(key, row_low, row_high):
    noise = jax.random.truncated_normal(key, -4.0, 4.0, (NDOF, NSNAP), jnp.float32)
    row_key = jax.random.fold_in(key, 17)
    row_scale = jnp.exp(jax.random.uniform(row_key, (NDOF, 1), jnp.float32, jnp.log(row_low), jnp.log(row_high) + 1e-06))
    column = jnp.arange(NSNAP, dtype=jnp.float32) / max(NSNAP - 1, 1)
    amplitude = jnp.exp(jnp.log(3.0) * column)[None, :]
    return (noise * row_scale * amplitude, amplitude)


def draw_snapshots(key, part):
    field, amplitude = shared_field(key, 1.0, 1.0)
    return field.astype(jnp.bfloat16)


def draw_derivatives(key, part):
    field, amplitude = shared_field(key, 1.0, 1.0)
    key = jax.random.fold_in(key, 5)
    rate_key, noise_key = jax.random.split(key)
    rates = jnp.exp(jax.random.uniform(rate_key, (NDOF, 1), jnp.float32, jnp.log(0.2), jnp.log(5.0)))
    extra = jax.random.truncated_normal(noise_key, -4.0, 4.0, (NDOF, NSNAP), jnp.float32)
    return (-rates * field + 0.5 * amplitude * extra).astype(jnp.bfloat16)


def scatter_about(own_key, extent, width, limit, kind=jnp.bfloat16):
    entries = jax.random.normal(own_key, extent, jnp.float32) * width
    return jnp.minimum(jnp.maximum(entries, -limit), limit).astype(kind)


def setup_inputs(seed: int = 0) -> dict:
    key_of = jax.random.split(jax.random.key(seed), 4)
    return {
        "snapshots": draw_snapshots(jax.random.fold_in(key_of[3], 71), 0),
        "derivatives": draw_derivatives(jax.random.fold_in(key_of[3], 71), 0),
        "basis": scatter_about(key_of[2], (NDOF, R), NDOF ** -0.5, 0.0625),
    }


def project(basis, field):
    return lax.dot_general(basis.astype(jnp.float32), field.astype(jnp.float32), (((0,), (0,)), ((), ())), preferred_element_type=jnp.float32)

def reference(snapshots, derivatives, basis):
    states = project(basis, snapshots)
    rates = project(basis, derivatives)
    count = states.shape[1]
    gram = jnp.dot(states, states.T, precision=lax.Precision.HIGHEST) / count
    gram = gram + 0.05 * jnp.eye(gram.shape[0], dtype=gram.dtype)
    cross = jnp.dot(rates, states.T, precision=lax.Precision.HIGHEST) / count
    factor = jnp.linalg.cholesky(gram)
    middle = lax.linalg.triangular_solve(factor, cross.T, left_side=True, lower=True)
    solved = lax.linalg.triangular_solve(factor, middle, left_side=True, lower=True, transpose_a=True)
    return (states, solved.T)
```

```python
import functools

import jax
import jax.numpy as jnp
from jax import lax
from jax.experimental import pallas as pl
from jax.experimental.pallas import tpu as pltpu
from jax.sharding import PartitionSpec as P

B = 128
PAN = 8
MESH = pl.DeviceIdType.MESH


def project(basis, field):
    return lax.dot_general(
        basis, field, (((0,), (0,)), ((), ())), preferred_element_type=jnp.float32
    )


def split(x):
    high = x.astype(jnp.bfloat16)
    return high, (x - high.astype(jnp.float32)).astype(jnp.bfloat16)


def dot3(a, b, dims):
    mul = lambda x, y: lax.dot_general(
        x, y, (dims, ((), ())), preferred_element_type=jnp.float32
    )
    return mul(a[0], b[0]) + (mul(a[0], b[1]) + mul(a[1], b[0]))


NN = ((1,), (0,))
NT = ((1,), (1,))


def reduce_kernel(nb, states_ref, rates_ref, out_ref, acc, got1, got2, got3, send, recv):
    r = nb * B
    low = [(i, j) for i in range(nb) for j in range(i + 1)]
    total = (len(low) + nb * nb) * B
    half, quarter, piece = total // 2, total // 8, total // 32

    me = lax.axis_index("tm")
    core = me % 2
    xy = (me // 2) % 4
    z = me // 8

    def dev(zz, qq, cc):
        return (0, zz * 8 + qq * 2 + cc)

    core_peer = dev(z, xy, 1 - core)
    flips = [xy + 1 - 2 * (xy % 2), lax.rem(xy + 2, 4)]
    flips.append(3 - xy)
    xy_peers = [dev(z, q, core) for q in flips]
    zs = [lax.rem(z + d, 4) for d in (1, 2, 3)]
    z_peers = [dev(q, xy, core) for q in zs]

    barrier = pltpu.get_barrier_semaphore()
    for peer in [core_peer] + xy_peers + z_peers:
        pl.semaphore_signal(barrier, inc=1, device_id=peer, device_id_type=MESH)
    pl.semaphore_wait(barrier, 7)

    s = split(states_ref[...])
    d = split(rates_ref[...])
    gram = dot3(s, s, NT)
    cross = dot3(d, s, NT)
    for n, (i, j) in enumerate(low):
        acc[n * B : (n + 1) * B, :] = gram[i * B : (i + 1) * B, j * B : (j + 1) * B]
    for j in range(nb):
        base = len(low) * B + j * r
        acc[base : base + r, :] = cross[:, j * B : (j + 1) * B]

    def rows(ref, start, size):
        return ref.at[pl.ds(pl.multiple_of(start, 8), size), :]

    def copy(n, src, dst, peer):
        c = pltpu.make_async_remote_copy(
            src_ref=src, dst_ref=dst, send_sem=send.at[n], recv_sem=recv.at[n],
            device_id=peer, device_id_type=MESH,
        )
        c.start()
        return c

    my_half = core * half
    my_quarter = my_half + xy * quarter
    my_piece = my_quarter + z * piece

    first = copy(0, rows(acc, (1 - core) * half, half), got1, core_peer)
    first.wait()
    acc[pl.ds(pl.multiple_of(my_half, 8), half), :] += got1[...]

    second = [
        copy(1 + k, rows(acc, my_half + q * quarter, quarter), got2.at[k], xy_peers[k])
        for k, q in enumerate(flips)
    ]
    for c in second:
        c.wait()
    acc[pl.ds(pl.multiple_of(my_quarter, 8), quarter), :] += got2[0] + got2[1] + got2[2]

    third = [
        copy(4 + k, rows(acc, my_quarter + q * piece, piece), got3.at[k], z_peers[k])
        for k, q in enumerate(zs)
    ]
    for c in third:
        c.wait()
    out_ref[pl.ds(pl.multiple_of(my_piece, 8), piece), :] = (
        acc[pl.ds(pl.multiple_of(my_piece, 8), piece), :] + got3[0] + got3[1] + got3[2]
    )

    part = rows(out_ref, my_piece, piece)
    fourth = [copy(7 + k, part, part, z_peers[k]) for k in range(3)]
    for c in fourth:
        c.wait()
    part5 = rows(out_ref, my_quarter, quarter)
    fifth = [copy(10 + k, part5, part5, xy_peers[k]) for k in range(3)]
    for c in fifth:
        c.wait()
    part6 = rows(out_ref, my_half, half)
    copy(13, part6, part6, core_peer).wait()


def reduce_sums(states, rates):
    nb = states.shape[0] // B
    total = (nb * (nb + 1) // 2 + nb * nb) * B
    f32 = jnp.float32
    vmem = pl.BlockSpec(memory_space=pltpu.VMEM)
    return pl.pallas_call(
        functools.partial(reduce_kernel, nb),
        out_shape=jax.ShapeDtypeStruct((total, B), f32),
        in_specs=[vmem] * 2,
        out_specs=vmem,
        scratch_shapes=[
            pltpu.VMEM((total, B), f32),
            pltpu.VMEM((total // 2, B), f32),
            pltpu.VMEM((3, total // 8, B), f32),
            pltpu.VMEM((3, total // 32, B), f32),
            pltpu.SemaphoreType.DMA((14,)),
            pltpu.SemaphoreType.DMA((14,)),
        ],
        compiler_params=pltpu.CompilerParams(
            collective_id=0, has_side_effects=True, vmem_limit_bytes=32 * 2**20
        ),
    )(states, rates)


def invert_block(block):
    tiles = [block[t * PAN : (t + 1) * PAN, :] for t in range(B // PAN)]
    lane = lax.broadcasted_iota(jnp.int32, (PAN, B), 1)
    sub = lax.broadcasted_iota(jnp.int32, (PAN, B), 0)
    wide = lambda x: jnp.broadcast_to(x, (PAN, B))
    for p in range(B // PAN):
        at = p * PAN
        inside = (lane >= at) & (lane < at + PAN)
        cols = [[wide(t[:, at + j : at + j + 1]) for j in range(PAN)] for t in tiles]
        diag = cols[p]
        u = jnp.where(inside, jnp.where(lane - at == sub, 1.0, 0.0), tiles[p])
        for k in range(PAN):
            hit = sub == k
            inv = 1.0 / wide(diag[k][k : k + 1, :])
            scale = jnp.where(hit, 0.0, diag[k])
            row = wide(u[k : k + 1, :]) * inv
            u = jnp.where(hit, row, u - scale * row)
            for j in range(k + 1, PAN):
                dj = wide(diag[j][k : k + 1, :]) * inv
                diag[j] = jnp.where(hit, dj, diag[j] - scale * dj)
        us = [wide(u[k : k + 1, :]) for k in range(PAN)]
        for t in [(p + 1 + q) % (B // PAN) for q in range(B // PAN)]:
            if t == p:
                tiles[t] = u
                continue
            new = jnp.where(inside, 0.0, tiles[t])
            for k in range(PAN):
                new = new - cols[t][k] * us[k]
            tiles[t] = new
    return jnp.concatenate(tiles, axis=0)


def solve_kernel(nb, count, sums_ref, out_ref):
    r = nb * B
    low = [(i, j) for i in range(nb) for j in range(i + 1)]
    diag = jnp.where(
        lax.broadcasted_iota(jnp.int32, (B, B), 0) == lax.broadcasted_iota(jnp.int32, (B, B), 1),
        0.05, 0.0,
    )
    g = {}
    for n, (i, j) in enumerate(low):
        g[i, j] = sums_ref[n * B : (n + 1) * B, :] * (1.0 / count)
        if i == j:
            g[i, j] = g[i, j] + diag
    c = []
    for j in range(nb):
        base = len(low) * B + j * r
        c.append(sums_ref[base : base + r, :] * (1.0 / count))
    low_factor, inverse = {}, []
    for j in range(nb):
        w = split(invert_block(g[j, j]))
        inverse.append(w)
        panel = {i: split(g[i, j]) for i in range(j + 1, nb)}
        for i in range(j + 1, nb):
            low_factor[i, j] = split(dot3(panel[i], w, NN))
        for i in range(j + 1, nb):
            for k in range(j + 1, i + 1):
                g[i, k] = g[i, k] - dot3(low_factor[i, j], panel[k], NT)
        c[j] = split(c[j])
        for k in range(j + 1, nb):
            c[k] = c[k] - dot3(c[j], low_factor[k, j], NT)
    x = [None] * nb
    for j in reversed(range(nb)):
        x[j] = dot3(c[j], inverse[j], NN)
        for i in range(j + 1, nb):
            x[j] = x[j] - dot3(x[i], low_factor[i, j], NN)
        out_ref[:, j * B : (j + 1) * B] = x[j]
        x[j] = split(x[j])


def solve_sums(sums, width, count):
    vmem = pl.BlockSpec(memory_space=pltpu.VMEM)
    return pl.pallas_call(
        functools.partial(solve_kernel, width // B, count),
        out_shape=jax.ShapeDtypeStruct((width, width), jnp.float32),
        in_specs=[vmem],
        out_specs=vmem,
        compiler_params=pltpu.CompilerParams(vmem_limit_bytes=32 * 2**20),
    )(sums)


def fast(snapshots, derivatives, basis):
    count = snapshots.shape[1] * lax.axis_size("tm")
    states = project(basis, snapshots)
    rates = project(basis, derivatives)
    sums = reduce_sums(states, rates)
    return states, solve_sums(sums, basis.shape[1], count)


def solve_rows(gram, cross_rows):
    factor = jnp.linalg.cholesky(gram)
    middle = lax.linalg.triangular_solve(factor, cross_rows.T, left_side=True, lower=True)
    solved = lax.linalg.triangular_solve(
        factor, middle, left_side=True, lower=True, transpose_a=True
    )
    return solved.T


def general(snapshots, derivatives, basis):
    count = snapshots.shape[1] * lax.axis_size("tm")
    width = basis.shape[1]
    rows = width // lax.axis_size("dof")
    start = lax.axis_index("dof") * rows
    local_states = project(basis, snapshots)
    local_rates = project(basis, derivatives)
    identity = 0.05 * jnp.eye(width, dtype=jnp.float32)
    states, rates = lax.psum((local_states, local_rates), "dof")
    gram_part = jnp.dot(states, states.T, precision=lax.Precision.HIGHEST)
    cross_part = jnp.dot(rates, states.T, precision=lax.Precision.HIGHEST)
    gram, cross = lax.psum((gram_part, cross_part), "tm")
    gram = gram / count + identity
    cross_rows = lax.dynamic_slice_in_dim(cross, start, rows, 0) / count
    state_out = lax.dynamic_slice_in_dim(states, start, rows, 0)
    return (state_out, solve_rows(gram, cross_rows))


def solution(mesh):
    placed = (P("dof", "tm"), P("dof", "tm"), P("dof", None))
    one = mesh.shape["dof"] == 1 and mesh.shape["tm"] == 32
    return jax.shard_map(
        fast if one else general,
        mesh=mesh,
        in_specs=placed,
        out_specs=(P("dof", "tm"), P("dof", None)),
        check_vma=False,
    )
```

```python
import functools

import jax
import jax.numpy as jnp
from jax import lax
from jax.experimental import pallas as pl
from jax.experimental.pallas import tpu as pltpu
from jax.sharding import PartitionSpec as P

B = 128
PAN = 8
MESH = pl.DeviceIdType.MESH


def project(basis, field):
    return lax.dot_general(
        basis, field, (((0,), (0,)), ((), ())), preferred_element_type=jnp.float32
    )


def split(x):
    high = x.astype(jnp.bfloat16)
    return high, (x - high.astype(jnp.float32)).astype(jnp.bfloat16)


def dot3(a, b, dims):
    mul = lambda x, y: lax.dot_general(
        x, y, (dims, ((), ())), preferred_element_type=jnp.float32
    )
    return mul(a[0], b[0]) + (mul(a[0], b[1]) + mul(a[1], b[0]))


NN = ((1,), (0,))
NT = ((1,), (1,))
TN = ((0,), (0,))


def project_kernel(fields_a, fields_b, basis, states_ref, rates_ref):
    @pl.when(pl.program_id(0) == 0)
    def _():
        states_ref[...] = jnp.zeros_like(states_ref)
        rates_ref[...] = jnp.zeros_like(rates_ref)

    n = fields_a.shape[0]
    both = jnp.concatenate([fields_a[...], fields_b[...]], axis=0)
    part = jnp.dot(both, basis[...], preferred_element_type=jnp.float32)
    states_ref[...] += part[:n]
    rates_ref[...] += part[n:]


def project_both(snapshots_t, derivatives_t, basis, chunk=1024):
    n, depth = snapshots_t.shape
    width = basis.shape[1]
    field = pl.BlockSpec((n, chunk), lambda i: (0, i))
    result = pl.BlockSpec((n, width), lambda i: (0, 0))
    return pl.pallas_call(
        project_kernel,
        grid=(depth // chunk,),
        out_shape=[jax.ShapeDtypeStruct((n, width), jnp.float32)] * 2,
        in_specs=[field, field, pl.BlockSpec((chunk, width), lambda i: (i, 0))],
        out_specs=[result, result],
        compiler_params=pltpu.CompilerParams(vmem_limit_bytes=56 * 2**20),
    )(snapshots_t, derivatives_t, basis)


def lower_blocks(nb):
    return [(i, j) for i in range(nb) for j in range(i + 1)]


def aligned(ref, start, size):
    return ref.at[pl.ds(pl.multiple_of(start, 8), size), :]


class AllReduce:
    def __init__(self, place, acc, out, got, send, recv):
        self.core, self.xy, self.z, self.peers = place
        self.acc, self.out, self.got, self.send, self.recv = acc, out, got, send, recv
        total = acc.shape[0]
        self.half, self.quarter, self.piece = total // 2, total // 8, total // 32
        self.my_half = self.core * self.half
        self.my_quarter = self.my_half + self.xy * self.quarter
        self.my_piece = self.my_quarter + self.z * self.piece
        self.flying = []

    def start(self, first, pairs, peers):
        for k, (src, dst) in enumerate(pairs):
            n = first + k
            c = pltpu.make_async_remote_copy(
                src_ref=src, dst_ref=dst, send_sem=self.send.at[n],
                recv_sem=self.recv.at[n], device_id=peers[k], device_id_type=MESH,
            )
            c.start()
            self.flying.append(c)

    def land(self):
        for c in self.flying:
            c.wait()
        self.flying = []

    def step(self, n):
        self.land()
        acc, out, got = self.acc, self.out, self.got
        core_peer, (flips, xy_peers), (zs, z_peers) = self.peers
        if n == 0:
            src = aligned(acc, (1 - self.core) * self.half, self.half)
            self.start(0, [(src, got[0])], [core_peer])
        elif n == 1:
            aligned(acc, self.my_half, self.half)[...] += got[0][...]
            self.start(1, [
                (aligned(acc, self.my_half + q * self.quarter, self.quarter), got[1].at[k])
                for k, q in enumerate(flips)
            ], xy_peers)
        elif n == 2:
            aligned(acc, self.my_quarter, self.quarter)[...] += (
                got[1][0] + got[1][1] + got[1][2]
            )
            self.start(4, [
                (aligned(acc, self.my_quarter + q * self.piece, self.piece), got[2].at[k])
                for k, q in enumerate(zs)
            ], z_peers)
        elif n == 3:
            part = aligned(out, self.my_piece, self.piece)
            part[...] = (
                aligned(acc, self.my_piece, self.piece)[...]
                + got[2][0] + got[2][1] + got[2][2]
            )
            self.start(7, [(part, part)] * 3, z_peers)
        elif n == 4:
            part = aligned(out, self.my_quarter, self.quarter)
            self.start(10, [(part, part)] * 3, xy_peers)
        elif n == 5:
            part = aligned(out, self.my_half, self.half)
            self.start(13, [(part, part)], [core_peer])


def invert_block(block, hook):
    np_ = B // PAN
    tiles = block.reshape(np_, PAN, B)
    lane = lax.broadcasted_iota(jnp.int32, (PAN, B), 1)
    sub = lax.broadcasted_iota(jnp.int32, (PAN, B), 0)
    wide = lambda x: jnp.broadcast_to(x, (PAN, B))
    for p in range(np_):
        hook(p)
        at = p * PAN
        inside = (lane >= at) & (lane < at + PAN)
        cols = [
            jnp.broadcast_to(tiles[:, :, at + j : at + j + 1], (np_, PAN, B))
            for j in range(PAN)
        ]
        diag = jnp.stack([c[p] for c in cols])
        u = jnp.where(inside, jnp.where(lane - at == sub, 1.0, 0.0), tiles[p])
        for k in range(PAN):
            hit = sub == k
            pivot = diag[0]
            inv = 1.0 / wide(pivot[k : k + 1, :])
            scale = jnp.where(hit, 0.0, pivot)
            row = wide(u[k : k + 1, :]) * inv
            u = jnp.where(hit, row, u - scale * row)
            if k < PAN - 1:
                diag = diag[1:]
                head = jnp.broadcast_to(diag[:, k : k + 1, :], diag.shape) * inv[None]
                diag = jnp.where(hit[None], head, diag - scale[None] * head)
        new = jnp.where(inside[None], 0.0, tiles)
        for k in range(PAN):
            new = new - cols[k] * wide(u[k : k + 1, :])[None]
        parts = [new[:p]] if p else []
        parts += [u[None]] + ([new[p + 1 :]] if p + 1 < np_ else [])
        tiles = jnp.concatenate(parts, axis=0)
    return tiles.reshape(B, B)


def factor_blocks(nb, count, sums_ref, out_ref, hook):
    diag = jnp.where(
        lax.broadcasted_iota(jnp.int32, (B, B), 0) == lax.broadcasted_iota(jnp.int32, (B, B), 1),
        0.05, 0.0,
    )
    index = {ij: n * B for n, ij in enumerate(lower_blocks(nb))}
    g = {}
    for (i, j), n in index.items():
        g[i, j] = sums_ref[n : n + B, :] * (1.0 / count)
        if i == j:
            g[i, j] = g[i, j] + diag
    for j in range(nb):
        w = invert_block(g[j, j], functools.partial(hook, j))
        out_ref[index[j, j] : index[j, j] + B, :] = w
        w = split(w)
        panel = {i: split(g[i, j]) for i in range(j + 1, nb)}
        for i in range(j + 1, nb):
            low = dot3(panel[i], w, NN)
            out_ref[index[i, j] : index[i, j] + B, :] = low
            low = split(low)
            for k in range(j + 1, i + 1):
                g[i, k] = g[i, k] - dot3(low, panel[k], NT)


def sums_kernel(
    nb, count, states_ref, rates_ref, factor_ref, cross_ref,
    acc_g, out_g, g0, g1, g2, acc_c, c0, c1, c2, send_g, recv_g, send_c, recv_c,
):
    r = nb * B
    me = lax.axis_index("tm")
    core, xy, z = me % 2, (me // 2) % 4, me // 8

    def dev(zz, qq, cc):
        return (0, zz * 8 + qq * 2 + cc)

    flips = [xy + 1 - 2 * (xy % 2), (xy + 2) % 4, 3 - xy]
    zs = [(z + d) % 4 for d in (1, 2, 3)]
    core_peer = dev(z, xy, 1 - core)
    xy_peers = [dev(z, q, core) for q in flips]
    z_peers = [dev(q, xy, core) for q in zs]
    place = (core, xy, z, (core_peer, (flips, xy_peers), (zs, z_peers)))

    barrier = pltpu.get_barrier_semaphore()
    for peer in [core_peer] + xy_peers + z_peers:
        pl.semaphore_signal(barrier, inc=1, device_id=peer, device_id_type=MESH)

    s = split(states_ref[...])
    gram = dot3(s, s, TN)
    for n, (i, j) in enumerate(lower_blocks(nb)):
        acc_g[n * B : (n + 1) * B, :] = gram[i * B : (i + 1) * B, j * B : (j + 1) * B]
    pl.semaphore_wait(barrier, 7)

    of_gram = AllReduce(place, acc_g, out_g, (g0, g1, g2), send_g, recv_g)
    of_cross = AllReduce(place, acc_c, cross_ref, (c0, c1, c2), send_c, recv_c)
    of_gram.step(0)
    d = split(rates_ref[...])
    cross = dot3(d, s, TN)
    for j in range(nb):
        acc_c[j * r : (j + 1) * r, :] = cross[:, j * B : (j + 1) * B]
    of_gram.step(1)
    of_cross.step(0)
    for n in range(2, 6):
        of_gram.step(n)
    of_cross.step(1)
    of_gram.land()

    steps = {(1, 0): 2, (1, B // PAN // 2): 3, (2, 0): 4, (3, 0): 5}

    def hook(j, p):
        if (j, p) in steps:
            of_cross.step(steps[j, p])

    factor_blocks(nb, count, out_g, factor_ref, hook)
    of_cross.land()


def sums_and_factor(states_t, rates_t, count):
    width = states_t.shape[1]
    nb = width // B
    f32 = jnp.float32
    gram, cross = nb * (nb + 1) // 2 * B, nb * nb * B
    vmem = pl.BlockSpec(memory_space=pltpu.VMEM)

    def landing(total):
        return [
            pltpu.VMEM((total // 2, B), f32),
            pltpu.VMEM((3, total // 8, B), f32),
            pltpu.VMEM((3, total // 32, B), f32),
        ]

    return pl.pallas_call(
        functools.partial(sums_kernel, nb, count),
        out_shape=[jax.ShapeDtypeStruct((gram, B), f32), jax.ShapeDtypeStruct((cross, B), f32)],
        in_specs=[vmem] * 2,
        out_specs=[vmem] * 2,
        scratch_shapes=[pltpu.VMEM((gram, B), f32)] * 2
        + landing(gram)
        + [pltpu.VMEM((cross, B), f32)]
        + landing(cross)
        + [pltpu.SemaphoreType.DMA((14,))] * 4,
        compiler_params=pltpu.CompilerParams(
            collective_id=0, has_side_effects=True, vmem_limit_bytes=32 * 2**20
        ),
    )(states_t, rates_t)


def substitute_kernel(nb, count, factor_ref, cross_ref, out_ref):
    r = nb * B
    index = {ij: n * B for n, ij in enumerate(lower_blocks(nb))}
    f = {ij: split(factor_ref[n : n + B, :]) for ij, n in index.items()}
    c = [cross_ref[j * r : (j + 1) * r, :] * (1.0 / count) for j in range(nb)]
    for j in range(nb):
        c[j] = split(c[j])
        for k in range(j + 1, nb):
            c[k] = c[k] - dot3(c[j], f[k, j], NT)
    x = [dot3(c[j], f[j, j], NN) for j in range(nb)]
    for j in reversed(range(nb)):
        out_ref[:, j * B : (j + 1) * B] = x[j]
        done = split(x[j])
        for k in range(j):
            x[k] = x[k] - dot3(done, f[j, k], NN)


def substitute(factor, cross, width, count):
    vmem = pl.BlockSpec(memory_space=pltpu.VMEM)
    return pl.pallas_call(
        functools.partial(substitute_kernel, width // B, count),
        out_shape=jax.ShapeDtypeStruct((width, width), jnp.float32),
        in_specs=[vmem] * 2,
        out_specs=vmem,
        compiler_params=pltpu.CompilerParams(vmem_limit_bytes=32 * 2**20),
    )(factor, cross)


def fast(snapshots, derivatives, basis):
    count = snapshots.shape[1] * lax.axis_size("tm")
    states_t, rates_t = project_both(snapshots.T, derivatives.T, basis)
    factor, cross = sums_and_factor(states_t, rates_t, count)
    return states_t.T, substitute(factor, cross, basis.shape[1], count)


def solve_rows(gram, cross_rows):
    factor = jnp.linalg.cholesky(gram)
    middle = lax.linalg.triangular_solve(factor, cross_rows.T, left_side=True, lower=True)
    solved = lax.linalg.triangular_solve(
        factor, middle, left_side=True, lower=True, transpose_a=True
    )
    return solved.T


def general(snapshots, derivatives, basis):
    count = snapshots.shape[1] * lax.axis_size("tm")
    width = basis.shape[1]
    rows = width // lax.axis_size("dof")
    start = lax.axis_index("dof") * rows
    local_states = project(basis, snapshots)
    local_rates = project(basis, derivatives)
    identity = 0.05 * jnp.eye(width, dtype=jnp.float32)
    states, rates = lax.psum((local_states, local_rates), "dof")
    gram_part = jnp.dot(states, states.T, precision=lax.Precision.HIGHEST)
    cross_part = jnp.dot(rates, states.T, precision=lax.Precision.HIGHEST)
    gram, cross = lax.psum((gram_part, cross_part), "tm")
    gram = gram / count + identity
    cross_rows = lax.dynamic_slice_in_dim(cross, start, rows, 0) / count
    state_out = lax.dynamic_slice_in_dim(states, start, rows, 0)
    return (state_out, solve_rows(gram, cross_rows))


def solution(mesh):
    placed = (P("dof", "tm"), P("dof", "tm"), P("dof", None))
    one = mesh.shape["dof"] == 1 and mesh.shape["tm"] == 32
    return jax.shard_map(
        fast if one else general,
        mesh=mesh,
        in_specs=placed,
        out_specs=(P("dof", "tm"), P("dof", None)),
        check_vma=False,
    )
```

```python
import functools

import jax
import jax.numpy as jnp
from jax import lax
from jax.experimental import pallas as pl
from jax.experimental.pallas import tpu as pltpu
from jax.sharding import PartitionSpec as P

B = 128
PAN = 8
MESH = pl.DeviceIdType.MESH


def project(basis, field):
    return lax.dot_general(
        basis, field, (((0,), (0,)), ((), ())), preferred_element_type=jnp.float32
    )


def split(x):
    high = x.astype(jnp.bfloat16)
    return high, (x - high.astype(jnp.float32)).astype(jnp.bfloat16)


def dot3(a, b, dims):
    mul = lambda x, y: lax.dot_general(
        x, y, (dims, ((), ())), preferred_element_type=jnp.float32
    )
    return mul(a[0], b[0]) + (mul(a[0], b[1]) + mul(a[1], b[0]))


NN = ((1,), (0,))
NT = ((1,), (1,))
TN = ((0,), (0,))


def project_kernel(fields_a, fields_b, basis, states_ref, both_ref):
    @pl.when(pl.program_id(0) == 0)
    def _():
        both_ref[...] = jnp.zeros_like(both_ref)

    both = jnp.concatenate([fields_a[...], fields_b[...]], axis=0)
    both_ref[...] += jnp.dot(both, basis[...], preferred_element_type=jnp.float32)

    @pl.when(pl.program_id(0) == pl.num_programs(0) - 1)
    def _():
        states_ref[...] = both_ref[: states_ref.shape[0], :]


def project_both(snapshots_t, derivatives_t, basis, chunk=2048):
    n, depth = snapshots_t.shape
    width = basis.shape[1]
    field = pl.BlockSpec((n, chunk), lambda i: (0, i))
    result = lambda rows: pl.BlockSpec((rows, width), lambda i: (0, 0))
    return pl.pallas_call(
        project_kernel,
        grid=(depth // chunk,),
        out_shape=[jax.ShapeDtypeStruct((k * n, width), jnp.float32) for k in (1, 2)],
        in_specs=[field, field, pl.BlockSpec((chunk, width), lambda i: (i, 0))],
        out_specs=[result(n), result(2 * n)],
        compiler_params=pltpu.CompilerParams(vmem_limit_bytes=56 * 2**20),
    )(snapshots_t, derivatives_t, basis)


def lower_blocks(nb):
    return [(i, j) for i in range(nb) for j in range(i + 1)]


def aligned(ref, start, size):
    return ref.at[pl.ds(pl.multiple_of(start, 8), size), :]


class AllReduce:
    def __init__(self, place, acc, out, got, send, recv):
        self.core, self.xy, self.z, self.peers = place
        self.acc, self.out, self.got, self.send, self.recv = acc, out, got, send, recv
        total = acc.shape[0]
        self.half, self.quarter, self.piece = total // 2, total // 8, total // 32
        self.my_half = self.core * self.half
        self.my_quarter = self.my_half + self.xy * self.quarter
        self.my_piece = self.my_quarter + self.z * self.piece
        self.flying = []

    def start(self, first, pairs, peers):
        for k, (src, dst) in enumerate(pairs):
            n = first + k
            c = pltpu.make_async_remote_copy(
                src_ref=src, dst_ref=dst, send_sem=self.send.at[n],
                recv_sem=self.recv.at[n], device_id=peers[k], device_id_type=MESH,
            )
            c.start()
            self.flying.append(c)

    def land(self):
        for c in self.flying:
            c.wait()
        self.flying = []

    def step(self, n):
        self.land()
        acc, out, got = self.acc, self.out, self.got
        core_peer, (flips, xy_peers), (zs, z_peers) = self.peers
        if n == 0:
            src = aligned(acc, (1 - self.core) * self.half, self.half)
            self.start(0, [(src, got[0])], [core_peer])
        elif n == 1:
            aligned(acc, self.my_half, self.half)[...] += got[0][...]
            self.start(1, [
                (aligned(acc, self.my_half + q * self.quarter, self.quarter), got[1].at[k])
                for k, q in enumerate(flips)
            ], xy_peers)
        elif n == 2:
            aligned(acc, self.my_quarter, self.quarter)[...] += (
                got[1][0] + got[1][1] + got[1][2]
            )
            self.start(4, [
                (aligned(acc, self.my_quarter + q * self.piece, self.piece), got[2].at[k])
                for k, q in enumerate(zs)
            ], z_peers)
        elif n == 3:
            part = aligned(out, self.my_piece, self.piece)
            part[...] = (
                aligned(acc, self.my_piece, self.piece)[...]
                + got[2][0] + got[2][1] + got[2][2]
            )
            self.start(7, [(part, part)] * 3, z_peers)
        elif n == 4:
            part = aligned(out, self.my_quarter, self.quarter)
            self.start(10, [(part, part)] * 3, xy_peers)
        elif n == 5:
            part = aligned(out, self.my_half, self.half)
            self.start(13, [(part, part)], [core_peer])


def invert_block(block, hook):
    np_ = B // PAN
    tiles = block.reshape(np_, PAN, B)
    lane = lax.broadcasted_iota(jnp.int32, (PAN, B), 1)
    sub = lax.broadcasted_iota(jnp.int32, (PAN, B), 0)
    wide = lambda x: jnp.broadcast_to(x, (PAN, B))
    for p in range(np_):
        hook(p)
        at = p * PAN
        inside = (lane >= at) & (lane < at + PAN)
        cols = [
            jnp.broadcast_to(tiles[:, :, at + j : at + j + 1], (np_, PAN, B))
            for j in range(PAN)
        ]
        diag = jnp.stack([c[p] for c in cols])
        u = jnp.where(inside, jnp.where(lane - at == sub, 1.0, 0.0), tiles[p])
        for k in range(PAN):
            hit = sub == k
            pivot = diag[0]
            inv = 1.0 / wide(pivot[k : k + 1, :])
            scale = jnp.where(hit, 0.0, pivot)
            row = wide(u[k : k + 1, :]) * inv
            u = jnp.where(hit, row, u - scale * row)
            if k < PAN - 1:
                diag = diag[1:]
                head = jnp.broadcast_to(diag[:, k : k + 1, :], diag.shape) * inv[None]
                diag = jnp.where(hit[None], head, diag - scale[None] * head)
        new = jnp.where(inside[None], 0.0, tiles)
        for k in range(PAN):
            new = new - cols[k] * wide(u[k : k + 1, :])[None]
        parts = [new[:p]] if p else []
        parts += [u[None]] + ([new[p + 1 :]] if p + 1 < np_ else [])
        tiles = jnp.concatenate(parts, axis=0)
    return tiles.reshape(B, B)


def factor_blocks(nb, count, sums_ref, out_ref, hook):
    diag = jnp.where(
        lax.broadcasted_iota(jnp.int32, (B, B), 0) == lax.broadcasted_iota(jnp.int32, (B, B), 1),
        0.05, 0.0,
    )
    index = {ij: n * B for n, ij in enumerate(lower_blocks(nb))}
    g = {}
    for (i, j), n in index.items():
        g[i, j] = sums_ref[n : n + B, :] * (1.0 / count)
        if i == j:
            g[i, j] = g[i, j] + diag
    for j in range(nb):
        w = invert_block(g[j, j], functools.partial(hook, j))
        out_ref[index[j, j] : index[j, j] + B, :] = w
        w = split(w)
        panel = {i: split(g[i, j]) for i in range(j + 1, nb)}
        for i in range(j + 1, nb):
            low = dot3(panel[i], w, NN)
            out_ref[index[i, j] : index[i, j] + B, :] = low
            low = split(low)
            for k in range(j + 1, i + 1):
                g[i, k] = g[i, k] - dot3(low, panel[k], NT)


def sums_kernel(
    nb, count, both_ref, factor_ref, cross_ref,
    acc_g, out_g, g0, g1, g2, acc_c, c0, c1, c2, send_g, recv_g, send_c, recv_c,
):
    r = nb * B
    me = lax.axis_index("tm")
    core, xy, z = me % 2, (me // 2) % 4, me // 8

    def dev(zz, qq, cc):
        return (0, zz * 8 + qq * 2 + cc)

    flips = [xy + 1 - 2 * (xy % 2), (xy + 2) % 4, 3 - xy]
    zs = [(z + d) % 4 for d in (1, 2, 3)]
    core_peer = dev(z, xy, 1 - core)
    xy_peers = [dev(z, q, core) for q in flips]
    z_peers = [dev(q, xy, core) for q in zs]
    place = (core, xy, z, (core_peer, (flips, xy_peers), (zs, z_peers)))

    barrier = pltpu.get_barrier_semaphore()
    for peer in [core_peer] + xy_peers + z_peers:
        pl.semaphore_signal(barrier, inc=1, device_id=peer, device_id_type=MESH)

    n_local = both_ref.shape[0] // 2
    s = split(both_ref[:n_local, :])
    gram = dot3(s, s, TN)
    for n, (i, j) in enumerate(lower_blocks(nb)):
        acc_g[n * B : (n + 1) * B, :] = gram[i * B : (i + 1) * B, j * B : (j + 1) * B]
    pl.semaphore_wait(barrier, 7)

    of_gram = AllReduce(place, acc_g, out_g, (g0, g1, g2), send_g, recv_g)
    of_cross = AllReduce(place, acc_c, cross_ref, (c0, c1, c2), send_c, recv_c)
    of_gram.step(0)
    of_gram.step(1)
    d = split(both_ref[n_local:, :])
    cross = dot3(d, s, TN)
    for j in range(nb):
        acc_c[j * r : (j + 1) * r, :] = cross[:, j * B : (j + 1) * B]
    of_cross.step(0)
    of_gram.step(2)
    of_gram.step(3)
    of_cross.step(1)
    of_gram.step(4)
    of_gram.step(5)
    of_cross.step(2)
    of_gram.land()

    steps = {(1, 0): 3, (2, 0): 4, (3, 0): 5}

    def hook(j, p):
        if (j, p) in steps:
            of_cross.step(steps[j, p])

    factor_blocks(nb, count, out_g, factor_ref, hook)
    of_cross.land()


def sums_and_factor(both_t, count):
    width = both_t.shape[1]
    nb = width // B
    f32 = jnp.float32
    gram, cross = nb * (nb + 1) // 2 * B, nb * nb * B
    vmem = pl.BlockSpec(memory_space=pltpu.VMEM)

    def landing(total):
        return [
            pltpu.VMEM((total // 2, B), f32),
            pltpu.VMEM((3, total // 8, B), f32),
            pltpu.VMEM((3, total // 32, B), f32),
        ]

    return pl.pallas_call(
        functools.partial(sums_kernel, nb, count),
        out_shape=[jax.ShapeDtypeStruct((gram, B), f32), jax.ShapeDtypeStruct((cross, B), f32)],
        in_specs=[vmem],
        out_specs=[vmem] * 2,
        scratch_shapes=[pltpu.VMEM((gram, B), f32)] * 2
        + landing(gram)
        + [pltpu.VMEM((cross, B), f32)]
        + landing(cross)
        + [pltpu.SemaphoreType.DMA((14,))] * 4,
        compiler_params=pltpu.CompilerParams(
            collective_id=0, has_side_effects=True, vmem_limit_bytes=32 * 2**20
        ),
    )(both_t)


def substitute_kernel(nb, count, factor_ref, cross_ref, out_ref):
    r = nb * B
    index = {ij: n * B for n, ij in enumerate(lower_blocks(nb))}
    f = {ij: split(factor_ref[n : n + B, :]) for ij, n in index.items()}
    c = [cross_ref[j * r : (j + 1) * r, :] * (1.0 / count) for j in range(nb)]
    for j in range(nb):
        c[j] = split(c[j])
        for k in range(j + 1, nb):
            c[k] = c[k] - dot3(c[j], f[k, j], NT)
    x = [dot3(c[j], f[j, j], NN) for j in range(nb)]
    for j in reversed(range(nb)):
        out_ref[:, j * B : (j + 1) * B] = x[j]
        done = split(x[j])
        for k in range(j):
            x[k] = x[k] - dot3(done, f[j, k], NN)


def substitute(factor, cross, width, count):
    vmem = pl.BlockSpec(memory_space=pltpu.VMEM)
    return pl.pallas_call(
        functools.partial(substitute_kernel, width // B, count),
        out_shape=jax.ShapeDtypeStruct((width, width), jnp.float32),
        in_specs=[vmem] * 2,
        out_specs=vmem,
        compiler_params=pltpu.CompilerParams(vmem_limit_bytes=32 * 2**20),
    )(factor, cross)


def fast(snapshots, derivatives, basis):
    count = snapshots.shape[1] * lax.axis_size("tm")
    states_t, both_t = project_both(snapshots.T, derivatives.T, basis)
    factor, cross = sums_and_factor(both_t, count)
    return states_t.T, substitute(factor, cross, basis.shape[1], count)


def solve_rows(gram, cross_rows):
    factor = jnp.linalg.cholesky(gram)
    middle = lax.linalg.triangular_solve(factor, cross_rows.T, left_side=True, lower=True)
    solved = lax.linalg.triangular_solve(
        factor, middle, left_side=True, lower=True, transpose_a=True
    )
    return solved.T


def general(snapshots, derivatives, basis):
    count = snapshots.shape[1] * lax.axis_size("tm")
    width = basis.shape[1]
    rows = width // lax.axis_size("dof")
    start = lax.axis_index("dof") * rows
    local_states = project(basis, snapshots)
    local_rates = project(basis, derivatives)
    identity = 0.05 * jnp.eye(width, dtype=jnp.float32)
    states, rates = lax.psum((local_states, local_rates), "dof")
    gram_part = jnp.dot(states, states.T, precision=lax.Precision.HIGHEST)
    cross_part = jnp.dot(rates, states.T, precision=lax.Precision.HIGHEST)
    gram, cross = lax.psum((gram_part, cross_part), "tm")
    gram = gram / count + identity
    cross_rows = lax.dynamic_slice_in_dim(cross, start, rows, 0) / count
    state_out = lax.dynamic_slice_in_dim(states, start, rows, 0)
    return (state_out, solve_rows(gram, cross_rows))


def solution(mesh):
    placed = (P("dof", "tm"), P("dof", "tm"), P("dof", None))
    one = mesh.shape["dof"] == 1 and mesh.shape["tm"] == 32
    return jax.shard_map(
        fast if one else general,
        mesh=mesh,
        in_specs=placed,
        out_specs=(P("dof", "tm"), P("dof", None)),
        check_vma=False,
    )
```
